32 devices in a mesh: bond: 8 (over z, core), row: 4 (over y, x).
Axes of the slice: x: 2, y: 2, z: 4, core: 2. Of those that a mesh axis runs over, the one named last changes fastest.
Arguments:
- left_core: float32 [8, 384, 2, 384], P('bond', 'row'), may hold values from -1 to 2
- right_core: float32 [8, 384, 2, 384], P('bond', 'row'), may hold values from -1 to 2
- gate_angles: float32 [8, 6], P('bond'), may hold values from -3.140625 to 3.140625
- sketch: float32 [768, 384], P('bond'), may hold values from -0.21875 to 0.21875
Outputs:
- next_pair: float32 [8, 768, 768], P('bond', 'row')
The draws below stay inside these ranges and needn't reach their ends.
All inputs are finite; a program needn't handle non-finite values.
Results may differ from the reference program's by a relative error of at most 0.0003.
Values sent between devices are 32-bit elements; how exact they have to be, the bound alone decides.
A program may use at most 64 MiB of HBM per device.

```python
import math
import jax
import jax.numpy as jnp
import numpy as np
from jax import lax

CHI = 384
ITERS = 2
BONDS = 8


def core_draw(key):
    noise_key, diag_key = jax.random.split(key)
    shape = (BONDS, CHI, 2, CHI)
    noise = jnp.clip(jax.random.normal(noise_key, shape, jnp.float32), -4.0, 4.0)
    diagonal = jax.random.uniform(diag_key, (BONDS, CHI, 2, 1), jnp.float32, 0.7, 1.3)
    identity = (lax.broadcasted_iota(jnp.int32, (CHI, CHI), 0) == lax.broadcasted_iota(jnp.int32, (CHI, CHI), 1)).astype(jnp.float32)
    return diagonal * identity[None, :, None, :] + 0.4 / math.sqrt(CHI) * noise


def draw_left_core(key, part):
    return core_draw(jax.random.fold_in(key, 11))


def draw_right_core(key, part):
    return core_draw(jax.random.fold_in(key, 23))


def shard_levels(key, shape, shards, smallest, largest):
    def one(position, parts):
        draws = jax.random.uniform(jax.random.fold_in(jax.random.fold_in(key, 6), position), (parts,), jnp.float32, smallest / len(shards), largest / len(shards))
        return jnp.repeat(jnp.exp(draws), shape[position] // parts).reshape((-1,) + (1,) * (len(shape) - position - 1))

    gain = one(*shards[0])
    for cut in shards[1:]:
        gain = gain * one(*cut)
    return gain


def scatter_about(rng, dims, deviation, reach, shards=(), kind=jnp.bfloat16):
    values = jax.random.normal(rng, dims, jnp.float32) * deviation
    if len(shards) > 0:
        values = shard_levels(rng, dims, shards, -0.22, 0.18) * values
    return jnp.clip(values, min=-reach, max=reach).astype(kind)


def setup_inputs(seed: int = 0) -> dict:
    keys = jax.random.split(jax.random.key(seed), 5)
    left_core = draw_left_core(jax.random.fold_in(keys[4], 71), 0)
    right_core = draw_right_core(jax.random.fold_in(keys[4], 71), 0)
    gate_angles = jnp.clip(jax.random.uniform(keys[2], (BONDS, 6), jnp.float32, -3.140625, 3.140625), -3.140625, 3.140625)
    sketch = scatter_about(keys[3], (2 * CHI, CHI), (2 * CHI) ** -0.5, 0.21875, ((0, 8),), jnp.float32)
    return dict(left_core=left_core, right_core=right_core, gate_angles=gate_angles, sketch=sketch)


HIGHEST = lax.Precision.HIGHEST
PLANES = ((0, 1), (2, 3), (0, 2), (1, 3), (0, 3), (1, 2))

def rotation(first_axis, second_axis, cosine, sine_value):
    unit = np.eye(4, dtype=np.float32)
    diag_part = np.outer(unit[first_axis], unit[first_axis]) + np.outer(unit[second_axis], unit[second_axis])
    skew_part = np.outer(unit[second_axis], unit[first_axis]) - np.outer(unit[first_axis], unit[second_axis])
    rest_part = np.eye(4, dtype=np.float32) - diag_part
    return jnp.asarray(rest_part) + cosine * jnp.asarray(diag_part) + sine_value * jnp.asarray(skew_part)

def build_gate(angles):
    gate_matrix = jnp.eye(4, dtype=jnp.float32)
    for number, plane in enumerate(PLANES):
        rotated = rotation(plane[0], plane[1], jnp.cos(angles[number]), jnp.sin(angles[number]))
        gate_matrix = jnp.dot(rotated.astype(jnp.float32), gate_matrix.astype(jnp.float32), precision=HIGHEST, preferred_element_type=jnp.float32)
    return gate_matrix

def apply_gate(two_site, gate_matrix):
    width = two_site.shape[1] // 2
    blocks = two_site.reshape(two_site.shape[0] // 2, 2, 2, width)
    mixed_gate = jnp.einsum('pqtu,atuc->apqc', gate_matrix.reshape(2, 2, 2, 2), blocks, precision=HIGHEST)
    return mixed_gate.reshape(two_site.shape)

def orthonormal(sketched):
    gram_matrix = jnp.dot(sketched.T.astype(jnp.float32), sketched.astype(jnp.float32), precision=HIGHEST, preferred_element_type=jnp.float32)
    chol_factor = jnp.linalg.cholesky(gram_matrix)
    return lax.linalg.triangular_solve(chol_factor, sketched, left_side=False, lower=True, transpose_a=True)

def reference(left_core, right_core, gate_angles, sketch):

    def one_bond(inputs):
        left_one, right_one, angles = inputs
        two_site = jnp.dot(left_one.reshape(2 * CHI, CHI).astype(jnp.float32), right_one.reshape(CHI, 2 * CHI).astype(jnp.float32), precision=HIGHEST, preferred_element_type=jnp.float32)
        two_site = apply_gate(two_site, build_gate(angles))
        ortho_basis = orthonormal(jnp.dot(two_site.astype(jnp.float32), sketch.astype(jnp.float32), precision=HIGHEST, preferred_element_type=jnp.float32))
        for repeat in range(ITERS):
            projected = jnp.dot(two_site.T.astype(jnp.float32), ortho_basis.astype(jnp.float32), precision=HIGHEST, preferred_element_type=jnp.float32)
            ortho_basis = orthonormal(jnp.dot(two_site.astype(jnp.float32), projected.astype(jnp.float32), precision=HIGHEST, preferred_element_type=jnp.float32))
        carried = jnp.dot(ortho_basis.T.astype(jnp.float32), two_site.astype(jnp.float32), precision=HIGHEST, preferred_element_type=jnp.float32)
        return (carried, ortho_basis)
    carried, bases = lax.map(one_bond, (left_core, right_core, gate_angles))
    incoming = jnp.concatenate([jnp.zeros((1, CHI, 2 * CHI), jnp.float32), carried[:-1]], 0)

    def finish(inputs):
        came_in, ortho_basis = inputs
        return jnp.dot(came_in.reshape(2 * CHI, CHI).astype(jnp.float32), ortho_basis.reshape(CHI, 2 * CHI).astype(jnp.float32), precision=HIGHEST, preferred_element_type=jnp.float32)
    return lax.map(finish, (incoming, bases))
```

```python
import functools

import jax
import jax.numpy as jnp
from jax import lax
from jax.experimental import pallas as pl
from jax.experimental.pallas import tpu as pltpu
from jax.sharding import PartitionSpec as P

ITERS = 2
HIGHEST = lax.Precision.HIGHEST
PLANES = ((0, 1), (2, 3), (0, 2), (1, 3), (0, 3), (1, 2))
BASE = 64
F32 = jnp.float32
BF16 = jnp.bfloat16
NN = (((1,), (0,)), ((), ()))
NT = (((1,), (1,)), ((), ()))
TN = (((0,), (0,)), ((), ()))
VMEM_LIMIT = 48 << 20


def build_gate(angles):
    cosines, sines = jnp.cos(angles), jnp.sin(angles)
    rows = [[jnp.float32(i == j) for j in range(4)] for i in range(4)]
    for number, (first, second) in enumerate(PLANES):
        c, s = cosines[number], sines[number]
        upper = [c * x - s * y for x, y in zip(rows[first], rows[second])]
        lower = [s * x + c * y for x, y in zip(rows[first], rows[second])]
        rows[first], rows[second] = upper, lower
    return jnp.stack([x for row in rows for x in row])


def full(a, b, dims):
    return lax.dot_general(a, b, dims, precision=HIGHEST, preferred_element_type=F32)


def split(x):
    high = x.astype(BF16)
    return high, (x - high.astype(F32)).astype(BF16)


def three(a, b, dims):
    dot = lambda x, y: lax.dot_general(x, y, dims, preferred_element_type=F32)
    return dot(a[0], b[0]) + (dot(a[0], b[1]) + dot(a[1], b[0]))


def inverse_factor_base(a):
    groups = BASE // 8
    lanes = 2 * BASE
    sub = lax.broadcasted_iota(jnp.int32, (8, lanes), 0)
    row = lax.broadcasted_iota(jnp.int32, (BASE, BASE), 0)
    unit = (row == lax.broadcasted_iota(jnp.int32, (BASE, BASE), 1)).astype(F32)
    w = jnp.concatenate([a, unit], axis=1)
    w = [w[8 * g : 8 * g + 8, :] for g in range(groups)]
    for g in range(groups):
        columns = [
            [jnp.broadcast_to(w[k][:, 8 * g + m : 8 * g + m + 1], (8, lanes)) for k in range(g, groups)]
            for m in range(8)
        ]
        for j in range(8):
            scale = lax.rsqrt(columns[j][0][j : j + 1, :])
            factors = [c * scale for c in columns[j]]
            factors[0] = jnp.where(sub > j, factors[0], 0.0)
            pivot_row = w[g][j : j + 1, :] * scale
            for m in range(j + 1, 8):
                other = factors[0][m : m + 1, :]
                for k in range(groups - g):
                    columns[m][k] = columns[m][k] - factors[k] * other
            for k in range(g, groups):
                w[k] = w[k] - factors[k - g] * pivot_row
            w[g] = jnp.where(sub == j, pivot_row, w[g])
    return jnp.concatenate([x[:, BASE:] for x in w], axis=0)


def inverse_factor_pair(a):
    x11 = inverse_factor_base(a[:BASE, :BASE])
    l21 = full(a[BASE:, :BASE], x11, NT)
    x22 = inverse_factor_base(a[BASE:, BASE:] - full(l21, l21, NT))
    x21 = -full(x22, full(l21, x11, NN), NN)
    top = jnp.concatenate([x11, jnp.zeros_like(x11)], axis=1)
    return jnp.concatenate([top, jnp.concatenate([x21, x22], axis=1)], axis=0)


def inverse_factor(a, x):
    n = a.shape[0]
    step = 2 * BASE
    x[...] = jnp.zeros_like(x)
    for start in range(0, n, step):
        here = slice(start, start + step)
        x[here, here] = inverse_factor_pair(a[here, here])
        if start + step < n:
            rest = slice(start + step, n)
            l21 = full(a[rest, here], x[here, here], NT)
            a[rest, here] = l21
            a[rest, rest] = a[rest, rest] - full(l21, l21, NT)
        if start > 0:
            past = slice(0, start)
            x[here, past] = -full(x[here, here], full(a[here, past], x[past, past], NN), NN)


def body(gate, place, left, right, sketch, basis, carried, gh, gl, th, tl, y, q, gram, inv):
    chi = left.shape[1]
    tile = chi // 2
    halves = [split(right[u]) for u in range(2)]
    for piece in range(chi // tile):
        rows = slice(piece * tile, piece * tile + tile)
        tops = [split(left[t, rows, :]) for t in range(2)]
        theta = [three(tops[t], halves[u], NN) for t in range(2) for u in range(2)]
        for p in range(2):
            for r in range(2):
                block = sum(gate[0, (2 * p + r) * 4 + k] * theta[k] for k in range(4))
                here = slice(p * chi + piece * tile, p * chi + piece * tile + tile)
                cols = slice(r * chi, r * chi + chi)
                gh[here, cols], gl[here, cols] = split(block)
    step = 128
    for start in range(0, 2 * chi, step):
        here = slice(start, start + step)
        th[here, :] = gh[:, here].T
        tl[here, :] = gl[:, here].T

    def times(high, low, operand, out):
        for start in range(0, 2 * chi, 2 * chi // 3):
            here = slice(start, start + 2 * chi // 3)
            out[here, :] = three((high[here, :], low[here, :]), operand, NN)

    def factor():
        for start in range(0, chi, step):
            here = slice(start, start + step)
            gram[here, : start + step] = full(y[:, here], y[:, : start + step], TN)
        inverse_factor(gram, inv)

    times(gh, gl, split(sketch[...]), y)
    for repeat in range(ITERS + 1):
        factor()
        q[...] = three(split(y[...]), split(inv[...]), NT)
        if repeat < ITERS:
            times(th, tl, split(q[...]), y)
            times(gh, gl, split(y[...]), y)
    for p in range(2):
        basis[p] = q[p * chi : p * chi + chi, :]
    count = carried.shape[1]
    mine = inv[pl.ds(pl.multiple_of(place[0, 0] * count, 8), count), :]
    mine = three(split(mine), split(y[...]), NT)
    mine = three(split(mine), (gh[...], gl[...]), NN)
    for r in range(2):
        carried[r] = mine[:, r * chi : r * chi + chi]


def last(incoming, basis, out):
    count = incoming.shape[1]
    chi = incoming.shape[2]
    shape = (2 * count, 2 * count)
    row, col = (lax.broadcasted_iota(jnp.int32, shape, axis) for axis in range(2))
    weave = ((row % 2) * count + row // 2 == col).astype(BF16)
    parts = split(jnp.concatenate([incoming[0], incoming[1]], axis=0))
    woven = [jnp.dot(weave, x, preferred_element_type=F32).astype(BF16) for x in parts]
    for p in range(2):
        out[:, p * chi : p * chi + chi] = three(woven, split(basis[p]), NN)


def from_behind(value, axis, steps):
    count = lax.axis_size(axis)
    initial, final = (max(0, -steps), min(count, count - steps))
    return lax.ppermute(value, axis, [(source, source + steps) for source in range(initial, final)])


def on_device(left_core, right_core, gate_angles, sketch):
    sites, chi = left_core.shape[1], left_core.shape[3]
    gate = build_gate(gate_angles[0]).reshape(1, 16)
    left = jnp.transpose(left_core[0], (1, 0, 2))
    right = jnp.transpose(right_core[0], (1, 0, 2))
    left = lax.all_gather(left, "row", axis=1, tiled=True)
    right = lax.all_gather(right, "row", axis=1, tiled=True)
    whole_sketch = lax.all_gather(sketch, "bond", axis=0, tiled=True)
    place = jnp.full((1, 1), lax.axis_index("row"), jnp.int32)
    vmem = pl.BlockSpec(memory_space=pltpu.VMEM)
    smem = pl.BlockSpec(memory_space=pltpu.SMEM)
    square = (2 * chi, 2 * chi)
    basis, carried = pl.pallas_call(
        body,
        out_shape=(
            jax.ShapeDtypeStruct((2, chi, chi), F32),
            jax.ShapeDtypeStruct((2, sites, chi), F32),
        ),
        in_specs=[smem, smem, vmem, vmem, vmem],
        out_specs=(vmem, vmem),
        scratch_shapes=[
            pltpu.VMEM(square, BF16),
            pltpu.VMEM(square, BF16),
            pltpu.VMEM(square, BF16),
            pltpu.VMEM(square, BF16),
            pltpu.VMEM((2 * chi, chi), F32),
            pltpu.VMEM((2 * chi, chi), F32),
            pltpu.VMEM((chi, chi), F32),
            pltpu.VMEM((chi, chi), F32),
        ],
        compiler_params=pltpu.CompilerParams(vmem_limit_bytes=VMEM_LIMIT),
        name="bases",
    )(gate, place, left, right, whole_sketch)
    incoming = from_behind(carried, "bond", 1)
    next_block = pl.pallas_call(
        last,
        out_shape=jax.ShapeDtypeStruct((2 * sites, 2 * chi), F32),
        in_specs=[vmem, vmem],
        out_specs=vmem,
        compiler_params=pltpu.CompilerParams(vmem_limit_bytes=VMEM_LIMIT),
        name="next_pair",
    )(incoming, basis)
    return next_block[None]


def solution(mesh):
    return jax.shard_map(
        on_device,
        mesh=mesh,
        in_specs=(
            P("bond", "row", None, None),
            P("bond", "row", None, None),
            P("bond", None),
            P("bond", None),
        ),
        out_specs=P("bond", "row", None),
        check_vma=False,
    )
```

```python
import functools

import jax
import jax.numpy as jnp
from jax import lax
from jax.experimental import pallas as pl
from jax.experimental.pallas import tpu as pltpu
from jax.sharding import PartitionSpec as P

ITERS = 2
HIGHEST = lax.Precision.HIGHEST
PLANES = ((0, 1), (2, 3), (0, 2), (1, 3), (0, 3), (1, 2))
BASE = 64
F32 = jnp.float32
BF16 = jnp.bfloat16
NN = (((1,), (0,)), ((), ()))
NT = (((1,), (1,)), ((), ()))
TN = (((0,), (0,)), ((), ()))
VMEM_LIMIT = 48 << 20


def build_gate(angles):
    cosines, sines = jnp.cos(angles), jnp.sin(angles)
    rows = [[jnp.float32(i == j) for j in range(4)] for i in range(4)]
    for number, (first, second) in enumerate(PLANES):
        c, s = cosines[number], sines[number]
        upper = [c * x - s * y for x, y in zip(rows[first], rows[second])]
        lower = [s * x + c * y for x, y in zip(rows[first], rows[second])]
        rows[first], rows[second] = upper, lower
    return jnp.stack([x for row in rows for x in row])


def full(a, b, dims):
    return lax.dot_general(a, b, dims, precision=HIGHEST, preferred_element_type=F32)


def split(x):
    high = x.astype(BF16)
    return high, (x - high.astype(F32)).astype(BF16)


def three(a, b, dims):
    dot = lambda x, y: lax.dot_general(x, y, dims, preferred_element_type=F32)
    return dot(a[0], b[0]) + (dot(a[0], b[1]) + dot(a[1], b[0]))


def product(a, b):
    return three(split(a), split(b), NN)


def inverse_factor_base(a):
    groups = BASE // 8
    lanes = 2 * BASE
    sub = lax.broadcasted_iota(jnp.int32, (8, lanes), 0)
    row = lax.broadcasted_iota(jnp.int32, (BASE, BASE), 0)
    unit = (row == lax.broadcasted_iota(jnp.int32, (BASE, BASE), 1)).astype(F32)
    w = jnp.concatenate([a, unit], axis=1)
    w = [w[8 * g : 8 * g + 8, :] for g in range(groups)]
    for g in range(groups):
        columns = [
            [jnp.broadcast_to(w[k][:, 8 * g + m : 8 * g + m + 1], (8, lanes)) for k in range(g, groups)]
            for m in range(8)
        ]
        for j in range(8):
            scale = lax.rsqrt(columns[j][0][j : j + 1, :])
            factors = [c * scale for c in columns[j]]
            factors[0] = jnp.where(sub > j, factors[0], 0.0)
            pivot_row = w[g][j : j + 1, :] * scale
            for m in range(j + 1, 8):
                other = factors[0][m : m + 1, :]
                for k in range(groups - g):
                    columns[m][k] = columns[m][k] - factors[k] * other
            for k in range(g, groups):
                w[k] = w[k] - factors[k - g] * pivot_row
            w[g] = jnp.where(sub == j, pivot_row, w[g])
    return jnp.concatenate([x[:, BASE:] for x in w], axis=0)


def inverse_factor_pair(a):
    x11 = inverse_factor_base(a[:BASE, :BASE])
    l21 = full(a[BASE:, :BASE], x11, NT)
    x22 = inverse_factor_base(a[BASE:, BASE:] - full(l21, l21, NT))
    x21 = -product(x22, product(l21, x11))
    top = jnp.concatenate([x11, jnp.zeros_like(x11)], axis=1)
    return jnp.concatenate([top, jnp.concatenate([x21, x22], axis=1)], axis=0)


def inverse_factor(a, x):
    n = a.shape[0]
    step = 2 * BASE
    x[...] = jnp.zeros_like(x)
    for start in range(0, n, step):
        here = slice(start, start + step)
        x[here, here] = inverse_factor_pair(a[here, here])
        if start + step < n:
            rest = slice(start + step, n)
            l21 = full(a[rest, here], x[here, here], NT)
            a[rest, here] = l21
            a[rest, rest] = a[rest, rest] - full(l21, l21, NT)
        if start > 0:
            past = slice(0, start)
            x[here, past] = -product(x[here, here], product(a[here, past], x[past, past]))


def body(gate, place, left, right, sketch, basis, carried, gh, gl, th, tl, y, q, gram, inv):
    chi = left.shape[1]
    tile = chi // 2
    halves = [split(right[u]) for u in range(2)]
    for piece in range(chi // tile):
        rows = slice(piece * tile, piece * tile + tile)
        tops = [split(left[t, rows, :]) for t in range(2)]
        theta = [three(tops[t], halves[u], NN) for t in range(2) for u in range(2)]
        for p in range(2):
            for r in range(2):
                block = sum(gate[0, (2 * p + r) * 4 + k] * theta[k] for k in range(4))
                here = slice(p * chi + piece * tile, p * chi + piece * tile + tile)
                cols = slice(r * chi, r * chi + chi)
                gh[here, cols], gl[here, cols] = split(block)
    step = 128
    for start in range(0, 2 * chi, step):
        here = slice(start, start + step)
        th[here, :] = gh[:, here].T
        tl[here, :] = gl[:, here].T

    def times(high, low, operand, out):
        for start in range(0, 2 * chi, 2 * chi // 3):
            here = slice(start, start + 2 * chi // 3)
            out[here, :] = three((high[here, :], low[here, :]), operand, NN)

    def factor():
        for start in range(0, chi, step):
            here = slice(start, start + step)
            gram[here, : start + step] = full(y[:, here], y[:, : start + step], TN)
        inverse_factor(gram, inv)

    times(gh, gl, split(sketch[...]), y)

    @pl.loop(0, ITERS + 1)
    def _(repeat):
        factor()
        q[...] = three(split(y[...]), split(inv[...]), NT)

        @pl.when(repeat < ITERS)
        def _():
            times(th, tl, split(q[...]), y)
            times(gh, gl, split(y[...]), y)

    for p in range(2):
        basis[p] = q[p * chi : p * chi + chi, :]
    count = carried.shape[1]
    mine = inv[pl.ds(pl.multiple_of(place[0, 0] * count, 8), count), :]
    mine = three(split(mine), split(y[...]), NT)
    mine = three(split(mine), (gh[...], gl[...]), NN)
    for r in range(2):
        carried[r] = mine[:, r * chi : r * chi + chi]


def last(incoming, basis, out):
    count = incoming.shape[1]
    chi = incoming.shape[2]
    shape = (2 * count, 2 * count)
    row, col = (lax.broadcasted_iota(jnp.int32, shape, axis) for axis in range(2))
    weave = ((row % 2) * count + row // 2 == col).astype(BF16)
    parts = split(jnp.concatenate([incoming[0], incoming[1]], axis=0))
    woven = [jnp.dot(weave, x, preferred_element_type=F32).astype(BF16) for x in parts]
    for p in range(2):
        out[:, p * chi : p * chi + chi] = three(woven, split(basis[p]), NN)


def gather(left, right, sketch, lefts, rights, sketches, local_sem, send_sem, recv_sem, far_send, far_recv, near_send, near_recv):
    count, total = lax.axis_size("row"), lax.axis_size("bond")
    chips = total // 2
    row, bond = lax.axis_index("row"), lax.axis_index("bond")
    chip, core = bond // 2, bond % 2
    sites, part = left.shape[1], sketch.shape[0]
    sibling = {"bond": chip * 2 + 1 - core}
    peers = [{"row": (row + d) % count} for d in range(1, count)]
    if count == 4:
        across = row + 1 - 2 * (row % 2)
        along = (row + 2) % 4
        peers = [{"row": across}, {"row": along}]
    far = [{"bond": (chip + d) % chips * 2 + core} for d in range(1, chips)]
    barrier = pltpu.get_barrier_semaphore()
    greeted = peers + far + [sibling]
    for peer in greeted:
        pl.semaphore_signal(barrier, inc=1, device_id=peer, device_id_type=pl.DeviceIdType.MESH)
    pl.semaphore_wait(barrier, len(greeted))

    def rows_of(index):
        return pl.ds(pl.multiple_of(index * sites, 8), sites)

    def part_of(index):
        return pl.ds(pl.multiple_of(index * part, 8), part)

    def remote(src, dst, send, recv, peer):
        copy = pltpu.make_async_remote_copy(
            src_ref=src, dst_ref=dst, send_sem=send, recv_sem=recv,
            device_id=peer, device_id_type=pl.DeviceIdType.MESH,
        )
        copy.start()
        return copy

    pairs = ((right, rights), (left, lefts))
    own = {}
    for number, (mine, whole) in enumerate(pairs):
        for half in range(2):
            for slot in ((half, 1 - half) if count == 4 else range(len(peers))):
                own[number, half, slot] = remote(
                    mine.at[half], whole.at[half, rows_of(row)],
                    send_sem.at[number, half, slot], recv_sem.at[number, half, slot], peers[slot],
                )
    distant = [
        remote(sketch, sketches.at[part_of(bond)], far_send.at[d], far_recv.at[d], peer)
        for d, peer in enumerate(far)
    ]
    near = [remote(sketch, sketches.at[part_of(bond)], near_send.at[0], near_recv.at[0], sibling)]
    here = []
    for number, (mine, whole) in enumerate(pairs):
        here.append(pltpu.make_async_copy(mine, whole.at[:, rows_of(row)], local_sem.at[number]))
    here.append(pltpu.make_async_copy(sketch, sketches.at[part_of(bond)], local_sem.at[2]))
    for copy in here:
        copy.start()
    waiting = []
    if count == 4:
        for number, (mine, whole) in enumerate(pairs):
            for half in range(2):
                own[number, half, half].wait_recv()
                block = whole.at[half, rows_of((across, along)[half])]
                waiting.append(remote(
                    block, block, send_sem.at[number, half, 2], recv_sem.at[number, half, 2], peers[1 - half],
                ))
    for d, copy in enumerate(distant):
        copy.wait_recv()
        block = sketches.at[part_of((chip + chips - 1 - d) % chips * 2 + core)]
        near.append(remote(block, block, near_send.at[d + 1], near_recv.at[d + 1], sibling))
    for (number, half, slot), copy in own.items():
        copy.wait_send()
        if count != 4 or slot != half:
            copy.wait_recv()
    for copy in distant:
        copy.wait_send()
    for copy in near + waiting + here:
        copy.wait()


def from_behind(value, axis, steps):
    count = lax.axis_size(axis)
    initial, final = (max(0, -steps), min(count, count - steps))
    return lax.ppermute(value, axis, [(source, source + steps) for source in range(initial, final)])


def on_device(left_core, right_core, gate_angles, sketch):
    sites, chi = left_core.shape[1], left_core.shape[3]
    gate = build_gate(gate_angles[0]).reshape(1, 16)
    left = jnp.transpose(left_core[0], (1, 0, 2))
    right = jnp.transpose(right_core[0], (1, 0, 2))
    rows, bonds = lax.axis_size("row"), lax.axis_size("bond")
    slots = max(3, rows - 1)
    dma = pltpu.SemaphoreType.DMA
    anywhere = pl.BlockSpec(memory_space=pl.ANY)
    left, right, whole_sketch = pl.pallas_call(
        gather,
        out_shape=(
            jax.ShapeDtypeStruct((2, chi, chi), F32),
            jax.ShapeDtypeStruct((2, chi, chi), F32),
            jax.ShapeDtypeStruct((2 * chi, chi), F32),
        ),
        in_specs=[anywhere] * 3,
        out_specs=(anywhere,) * 3,
        scratch_shapes=[
            dma((3,)),
            dma((2, 2, slots)),
            dma((2, 2, slots)),
            dma((bonds // 2,)),
            dma((bonds // 2,)),
            dma((bonds // 2,)),
            dma((bonds // 2,)),
        ],
        compiler_params=pltpu.CompilerParams(collective_id=0, has_side_effects=True),
        name="gather",
    )(left, right, sketch)
    place = jnp.full((1, 1), lax.axis_index("row"), jnp.int32)
    vmem = pl.BlockSpec(memory_space=pltpu.VMEM)
    smem = pl.BlockSpec(memory_space=pltpu.SMEM)
    square = (2 * chi, 2 * chi)
    basis, carried = pl.pallas_call(
        body,
        out_shape=(
            jax.ShapeDtypeStruct((2, chi, chi), F32),
            jax.ShapeDtypeStruct((2, sites, chi), F32),
        ),
        in_specs=[smem, smem, vmem, vmem, vmem],
        out_specs=(vmem, vmem),
        scratch_shapes=[
            pltpu.VMEM(square, BF16),
            pltpu.VMEM(square, BF16),
            pltpu.VMEM(square, BF16),
            pltpu.VMEM(square, BF16),
            pltpu.VMEM((2 * chi, chi), F32),
            pltpu.VMEM((2 * chi, chi), F32),
            pltpu.VMEM((chi, chi), F32),
            pltpu.VMEM((chi, chi), F32),
        ],
        compiler_params=pltpu.CompilerParams(vmem_limit_bytes=VMEM_LIMIT),
        name="bases",
    )(gate, place, left, right, whole_sketch)
    incoming = from_behind(carried, "bond", 1)
    next_block = pl.pallas_call(
        last,
        out_shape=jax.ShapeDtypeStruct((2 * sites, 2 * chi), F32),
        in_specs=[vmem, vmem],
        out_specs=vmem,
        compiler_params=pltpu.CompilerParams(vmem_limit_bytes=VMEM_LIMIT),
        name="next_pair",
    )(incoming, basis)
    return next_block[None]


def solution(mesh):
    return jax.shard_map(
        on_device,
        mesh=mesh,
        in_specs=(
            P("bond", "row", None, None),
            P("bond", "row", None, None),
            P("bond", None),
            P("bond", None),
        ),
        out_specs=P("bond", "row", None),
        check_vma=False,
    )
```
